256 devices in a mesh: col: 16 (over x_hi, y, core), row: 16 (over z, x_lo).
Axes of the slice: x: 4 (x_hi: 2, x_lo: 2; x = x_hi * 2 + x_lo), y: 4, z: 8, core: 2. Of those that a mesh axis runs over, the one named last changes fastest.
Arguments:
- inverse_root: float32 [4096, 4096], P('row', 'col'), as said below
- factor: float32 [4096, 16384], P('row', 'col'), may hold values from -0.09375 to 0.09375
- structure: int32 [32, 64], P('row', 'col'), may hold values from 0 to 1, as said below
- supernode: int32 [16384], P('col'), may hold values from 0 to 63, as said below
- pivot_inverse: float32 [16384, 1024], P(('col', 'row')), as said below
Outputs:
- offdiag: float32 [4096, 16384], P('row', 'col')
- diag_inverse: float32 [16384, 1024], P(('col', 'row'))
The draws below stay inside these ranges and needn't reach their ends.
Inputs may be any that keep to these rules, and one draw needn't show every extreme that they name: `inverse_root`: exactly symmetric. A supernode's columns are consecutive, lie within one block of 1024 columns, and number 256 to 1024 in multiples of 256; the numbers in block p start at 4 p and rise by one per supernode. Supernodes of 256 and of 1024 columns occur in every draw. `structure`: equal for all column groups of one supernode. `pivot_inverse`: each block of 1024 rows is symmetric and zero between columns of different supernodes.
All inputs are finite; a program needn't handle non-finite values.
Results may differ from the reference program's by a relative error of at most 0.00007.
Values sent between devices are 32-bit elements; how exact they have to be, the bound alone decides.
No kernel may reach another device: no remote copies, remote signals or barrier semaphores. Data moves between devices by JAX's collectives and lax.ppermute only.
A program may use at most 64 MiB of HBM per device.

```python
import jax
import jax.numpy as jnp
from jax import lax

NS = 4096
GRAIN = 256
BLK = 128
W_DEV = 1024
W = 16384


def grain_labels(key):
    columns = W // (4 * GRAIN)
    cuts = jax.random.randint(key, (columns, 3), 0, 2).astype(jnp.int32)
    cuts = cuts.at[0].set(0)
    cuts = cuts.at[columns - 1].set(1)
    local = jnp.concatenate([jnp.zeros((columns, 1), jnp.int32), jnp.cumsum(cuts, axis=1).astype(jnp.int32)], axis=1)
    labels = local + 4 * jnp.arange(columns, dtype=jnp.int32)[:, None]
    return labels.reshape(-1).astype(jnp.int32)


def draw_supernode(key, part):
    labels = grain_labels(key)
    return jnp.repeat(labels, GRAIN).astype(jnp.int32)


def draw_structure(key, part):
    labels = grain_labels(key)
    key = jax.random.fold_in(key, 5)
    first, second = jax.random.split(key)
    level = jax.random.randint(first, (W // GRAIN,), 1, 5)
    picks = jax.random.randint(second, (NS // BLK, W // GRAIN), 0, 4)
    bits = (picks < level[None, :]).astype(jnp.int32)
    return jnp.take(bits, labels, axis=1).astype(jnp.int32)


def draw_inverse_root(key, part):
    key = jax.random.fold_in(key, 11)
    first, second = jax.random.split(key)
    noise = jax.random.normal(first, (NS, NS), jnp.float32)
    sym = jnp.clip((noise + noise.T) * 0.7, -3.5, 3.5)
    eye = jnp.eye(NS, dtype=jnp.float32)
    diag = 2.0 + jax.random.uniform(second, (NS,), jnp.float32)
    return sym * (1.0 - eye) + eye * diag[None, :]


def draw_pivot_inverse(key, part):
    labels = jnp.repeat(grain_labels(key), GRAIN)
    key = jax.random.fold_in(key, 17)
    first, second = jax.random.split(key)
    blocks = W // W_DEV
    noise = jax.random.normal(first, (blocks, W_DEV, W_DEV), jnp.float32)
    sym = jnp.clip((noise + jnp.swapaxes(noise, 1, 2)) * 0.3, -1.5, 1.5)
    grouped = labels.reshape(blocks, W_DEV)
    same = (grouped[:, :, None] == grouped[:, None, :]).astype(jnp.float32)
    eye = jnp.eye(W_DEV, dtype=jnp.float32)[None, :, :]
    diag = 2.0 + jax.random.uniform(second, (blocks, 1, W_DEV), jnp.float32)
    whole = sym * same * (1.0 - eye) + eye * diag
    return whole.reshape(W, W_DEV)


def block_levels(rng, dims, pieces, least, high):
    gain, own = 1.0, jax.random.fold_in(rng, 6)
    for dim, blocks in pieces:
        heights = jnp.exp(jax.random.uniform(jax.random.fold_in(own, dim), (blocks,), jnp.float32, least / len(pieces), high / len(pieces)))
        gain = gain * jnp.repeat(heights, dims[dim] // blocks).reshape([-1 if axis == dim else 1 for axis in range(len(dims))])
    return gain


def scatter_about(stream_key, shape, scale, reach, shards=(), held_as=jnp.bfloat16):
    entries = scale * jax.random.normal(stream_key, shape, jnp.float32)
    if shards:
        entries = entries * block_levels(stream_key, shape, shards, -0.22, 0.18)
    return jnp.clip(entries, -reach, reach).astype(held_as)


def setup_inputs(seed: int = 0) -> dict:
    splits = jax.random.split(jax.random.key(seed), 6)
    return {
        "inverse_root": draw_inverse_root(jax.random.fold_in(splits[5], 71), 0),
        "factor": scatter_about(splits[1], (NS, W), NS ** -0.5, 0.09375, ((0, 16), (1, 16)), jnp.float32),
        "structure": draw_structure(jax.random.fold_in(splits[5], 71), 0),
        "supernode": draw_supernode(jax.random.fold_in(splits[5], 71), 0),
        "pivot_inverse": draw_pivot_inverse(jax.random.fold_in(splits[5], 71), 0),
    }


def reference(inverse_root, factor, structure, supernode, pivot_inverse):
    mask = jnp.repeat(jnp.repeat(structure, BLK, axis=0), GRAIN, axis=1).astype(jnp.float32)
    masked = factor * mask
    offdiag = -jnp.dot(inverse_root, masked, precision=lax.Precision.HIGHEST, preferred_element_type=jnp.float32) * mask
    blocks = W // W_DEV
    left = jnp.transpose(masked.reshape(NS, blocks, W_DEV), (1, 0, 2))
    right = jnp.transpose(offdiag.reshape(NS, blocks, W_DEV), (1, 0, 2))

    def diagonal_block(pair):
        return lax.dot_general(pair[0], pair[1], (((0,), (0,)), ((), ())), precision=lax.Precision.HIGHEST, preferred_element_type=jnp.float32)

    products = lax.map(diagonal_block, (left, right))
    labels = supernode.reshape(blocks, W_DEV)
    same = (labels[:, :, None] == labels[:, None, :]).astype(jnp.float32)
    diag_inverse = pivot_inverse.reshape(blocks, W_DEV, W_DEV) - products * same
    return offdiag, diag_inverse.reshape(W, W_DEV)
```

```python
import jax
import jax.numpy as jnp
from jax import lax
from jax.sharding import PartitionSpec as P

AXES = ("col", "row")
ROWS = 256
HALF = 512
HIGH = lax.Precision.HIGH


def place(index):
    c, r = divmod(index, 16)
    return c >> 3, (c >> 1) & 3, c & 1, r >> 1, r & 1


def index_of(xh, y, core, z, xl):
    return ((xh * 4 + y) * 2 + core) * 16 + z * 2 + xl


def pairs(move):
    return [(i, index_of(*move(*place(i)))) for i in range(256)]


def along_z(k):
    return pairs(lambda xh, y, core, z, xl: (xh, y, core, (z + k) % 8, xl))


def along_plane(k, first):
    def move(xh, y, core, z, xl):
        if (core == 0) == first:
            return xh, (y + k) % 4, core, z, xl
        x = (xh * 2 + xl + k) % 4
        return x >> 1, y, core, z, x & 1

    return pairs(move)


def to_work(s):
    return pairs(lambda xh, y, core, z, xl: (xh, y, s ^ xl, z, core))


def to_home(s):
    return [(b, a) for a, b in to_work(s)]


CORES = pairs(lambda xh, y, core, z, xl: (xh, y, 1 - core, z, xl))


def send(value, perm):
    return lax.ppermute(value, AXES, perm)


def dot(a, b):
    return jnp.dot(a, b, precision=HIGH, preferred_element_type=jnp.float32)


def dot_t(a, b):
    return lax.dot_general(
        a, b, (((0,), (0,)), ((), ())), precision=HIGH, preferred_element_type=jnp.float32
    )


def shards(inverse_root, factor, structure, supernode, pivot_inverse):
    col, row = lax.axis_index("col"), lax.axis_index("row")
    core, y, xh = col & 1, (col >> 1) & 3, col >> 3
    xl, z = row & 1, row >> 1
    x = xh * 2 + xl

    spread = structure.astype(jnp.float32)[:, None, :, None]
    mask = jnp.broadcast_to(spread, (2, 128, 4, 256)).reshape(256, 1024)
    masked = factor * mask

    own = []
    for s in range(2):
        half = lax.dynamic_slice(masked, (0, (xl ^ s) * HALF), (ROWS, HALF))
        own.append(send(half, to_work(s)))
    other = [send(own[1 - s], CORES) for s in range(2)]

    first = [inverse_root] + [send(inverse_root, along_plane(-k, True)) for k in (1, 2, 3)]
    line = jnp.stack(first)
    second = [line] + [send(line, along_plane(-k, False)) for k in (1, 2, 3)]
    near = jnp.concatenate(second)
    far = send(near, CORES)

    def root_block(zk, p):
        blocks = near if p == 0 else far
        holder = core ^ p
        dy = ((zk & 3) - y) & 3
        parts = []
        for s in range(2):
            dx = ((zk >> 2) * 2 + (s ^ core) - x) & 3
            at = jnp.where(holder == 0, dx * 4 + dy, dy * 4 + dx)
            parts.append(lax.dynamic_slice(blocks, (at, 0, 0), (1, ROWS, ROWS))[0])
        return jnp.concatenate(parts)

    total = dot(root_block(z, 0), own[0]) + dot(root_block(z, 1), own[1])
    held = {(1, 0): own[0], (1, 1): own[1], (-1, 0): own[0], (-1, 1): own[1]}
    for step in range(1, 5):
        for way in (1, -1):
            for p in range(2):
                if step == 4 and (way == 1) != (p == 0):
                    continue
                held[way, p] = send(held[way, p], along_z(way))
                zk = (z - way * step) & 7
                total = total + dot(root_block(zk, p), held[way, p])

    out = [send(total[s * ROWS : (s + 1) * ROWS], to_home(s)) for s in range(2)]
    product = jnp.where(
        xl == 0,
        jnp.concatenate([out[0], out[1]], axis=1),
        jnp.concatenate([out[1], out[0]], axis=1),
    )
    offdiag = -product * mask

    same_half = dot_t(jnp.concatenate(own), total)
    cross_half = dot_t(jnp.concatenate(other), total)
    terms = jnp.where(
        core == 0,
        jnp.concatenate([same_half, cross_half]),
        jnp.concatenate([cross_half, same_half]),
    )

    def term(zk):
        return lax.dynamic_slice(terms, (((zk + 16) & 7) * 128, 0), (128, HALF))

    up = term(z + 4)
    for step in range(1, 5):
        up = send(up, along_z(1))
        if step < 4:
            up = up + term(z + 4 - step)
    down = term(z - 3)
    for step in range(1, 4):
        down = send(down, along_z(-1))
        if step < 3:
            down = down + term(z - 3 + step)
    shares = up + down + term(z)
    back = []
    for s in range(2):
        piece = lax.dynamic_slice(shares, ((s ^ core) * 64, 0), (64, HALF))
        back.append(send(piece, to_home(s)))
    sums = jnp.where(
        xl == 0,
        jnp.concatenate([back[0], back[1]], axis=1),
        jnp.concatenate([back[1], back[0]], axis=1),
    )
    labels = lax.dynamic_slice(supernode, (row * 64,), (64,))
    same = labels[:, None] == supernode[None, :]
    return offdiag, pivot_inverse + jnp.where(same, sums, 0.0)


def solution(mesh):
    in_specs = (
        P("row", "col"),
        P("row", "col"),
        P("row", "col"),
        P("col"),
        P(("col", "row"), None),
    )
    out_specs = (P("row", "col"), P(("col", "row"), None))
    return jax.shard_map(shards, mesh=mesh, in_specs=in_specs, out_specs=out_specs, check_vma=False)
```

```python
import jax
import jax.numpy as jnp
from jax import lax
from jax.experimental import pallas as pl
from jax.experimental.pallas import tpu as pltpu
from jax.sharding import PartitionSpec as P

AXES = ("col", "row")
ROWS = 256
HIGH = lax.Precision.HIGH


def place(index):
    c, r = divmod(index, 16)
    return c >> 3, (c >> 1) & 3, c & 1, r >> 1, r & 1


def index_of(xh, y, core, z, xl):
    return ((xh * 4 + y) * 2 + core) * 16 + z * 2 + xl


def pairs(move, some=lambda xh, y, core, z, xl: True):
    return [(i, index_of(*move(*place(i)))) for i in range(256) if some(*place(i))]


def ring(way):
    return pairs(
        lambda xh, y, core, z, xl: (xh, y, core, (z + (way if core == 0 else -way)) % 8, xl)
    )


def along_plane(k, axis):
    def move(xh, y, core, z, xl):
        if core == axis:
            return xh, (y + k) % 4, core, z, xl
        x = (xh * 2 + xl + k) % 4
        return x >> 1, y, core, z, x & 1

    return pairs(move)


def to_home(way):
    return pairs(
        lambda xh, y, core, z, xl: (xh, y, xl, (z + (way if core == 0 else -way)) % 8, core)
    )


def swap_cores(some=lambda xh, y, core, z, xl: True):
    return pairs(lambda xh, y, core, z, xl: (xh, y, 1 - core, z, xl), some)


def send(value, perm):
    return lax.ppermute(value, AXES, perm)


def dot(a, b):
    return jnp.dot(a, b, precision=HIGH, preferred_element_type=jnp.float32)


TILE = 256


def split(value):
    high = value.astype(jnp.bfloat16)
    return high, (value - high.astype(jnp.float32)).astype(jnp.bfloat16)


def product_kernel(count, at_ref, near_ref, *refs):
    blocks, out_ref, left_high, left_low = refs[:count], *refs[count:]

    @pl.when(pl.program_id(0) == 0)
    def _():
        for b in range(count):
            for s in range(2):
                high, low = split(near_ref[at_ref[2 * b + s]])
                left_high[pl.ds(s * ROWS, ROWS), pl.ds(b * ROWS, ROWS)] = high
                left_low[pl.ds(s * ROWS, ROWS), pl.ds(b * ROWS, ROWS)] = low

    parts = [split(block[...]) for block in blocks]
    high = jnp.concatenate([part[0] for part in parts])
    low = jnp.concatenate([part[1] for part in parts])

    def mul(a, b):
        return jnp.dot(a, b, preferred_element_type=jnp.float32)

    out_ref[...] = (
        mul(left_high[...], low) + mul(left_low[...], high) + mul(left_high[...], high)
    )


def products(at, near, blocks):
    count = len(blocks)
    columns = blocks[0].shape[1]
    return pl.pallas_call(
        lambda *refs: product_kernel(count, *refs),
        grid_spec=pltpu.PrefetchScalarGridSpec(
            num_scalar_prefetch=1,
            grid=(columns // TILE,),
            in_specs=[pl.BlockSpec(near.shape, lambda j, at: (0, 0, 0), pipeline_mode=pl.Buffered(1))]
            + [pl.BlockSpec((ROWS, TILE), lambda j, at: (0, j))] * count,
            out_specs=pl.BlockSpec((2 * ROWS, TILE), lambda j, at: (0, j)),
            scratch_shapes=[pltpu.VMEM((2 * ROWS, count * ROWS), jnp.bfloat16)] * 2,
        ),
        out_shape=jax.ShapeDtypeStruct((2 * ROWS, columns), jnp.float32),
        compiler_params=pltpu.CompilerParams(vmem_limit_bytes=24 * 2**20),
        cost_estimate=pl.CostEstimate(
            flops=6 * 2 * ROWS * count * ROWS * columns,
            bytes_accessed=4 * (near.size + count * ROWS * columns + 2 * ROWS * columns),
            transcendentals=0,
        ),
    )(at, near, *blocks)


def shards(inverse_root, factor, structure, supernode, pivot_inverse):
    col, row = lax.axis_index("col"), lax.axis_index("row")
    core, y, xh = col & 1, (col >> 1) & 3, col >> 3
    xl, z = row & 1, row >> 1
    x = xh * 2 + xl
    never = z < 0
    way = 1 - 2 * core

    def after(value, earlier):
        corner = (1,) * (value.ndim - 2) + (8, 128)
        tile = lax.slice(value, (0,) * value.ndim, corner)
        for array in earlier:
            other = lax.slice(array, (0,) * array.ndim, (1,) * (array.ndim - 2) + (8, 128))
            tile = jnp.where(never, other.reshape(corner), tile)
        return lax.dynamic_update_slice(value, tile, (0,) * value.ndim)

    spread = structure.astype(jnp.float32)[:, None, :, None]
    mask = jnp.broadcast_to(spread, (2, 128, 4, 256)).reshape(256, 1024)
    masked = factor * mask

    own = send(masked, to_home(0))
    block = after(inverse_root, [own])
    around = [send(block, along_plane(-k, 0)) for k in (1, 2, 3)]
    line = jnp.stack([block] + around)
    ahead = [own, after(send(own, ring(1)), around)]
    astern = [own, after(send(own, ring(-1)), around)]
    beside = [send(line, along_plane(-1, 1)), None, send(line, along_plane(-3, 1))]
    ahead.append(after(send(ahead[1], ring(1)), beside[0::2]))
    astern.append(after(send(astern[1], ring(-1)), beside[0::2]))
    beside[1] = send(after(line, beside[0::2]), along_plane(-2, 1))
    ahead.append(after(send(ahead[2], ring(1)), beside[1:2]))
    astern.append(after(send(astern[2], ring(-1)), beside[1:2]))
    near = jnp.concatenate([line] + beside)

    def root_at(zk, s):
        dy = ((zk & 3) - y) & 3
        dx = (((zk & 7) >> 2) * 2 + s - x) & 3
        return jnp.where(core == 0, dx * 4 + dy, dy * 4 + dx)

    last = send(ahead[3][: ROWS // 2], ring(1))
    last_astern = send(astern[3][ROWS // 2 :], ring(-1))
    other = send(after(own, [ahead[3], astern[3]]), swap_cores())
    columns = jnp.where(
        core == 0, jnp.concatenate([own, other]), jnp.concatenate([other, own])
    ).T
    places = [z, z - way, z + way, z - way * 2, z + way * 2, z - way * 3, z + way * 3]
    at = jnp.stack([root_at(zk, s) for zk in places for s in range(2)])
    total = products(
        at.astype(jnp.int32),
        near,
        [own, ahead[1], astern[1], ahead[2], astern[2], ahead[3], astern[3]],
    )
    opposite = jnp.concatenate(
        [
            lax.dynamic_slice(near, (root_at(z + 4, s), 0, 0), (1, ROWS, ROWS))[0]
            for s in range(2)
        ]
    )

    total = total + dot(opposite, jnp.concatenate([last, last_astern]))
    total = total + send(total, swap_cores())

    def term(zk):
        at = (zk & 7) * 128 + core * 64
        return dot(lax.dynamic_slice(columns, (at, 0), (64, 2 * ROWS)), total)

    def step_of(far_sum, near_sum, step):
        arrived = [send(far_sum, ring(1)), send(near_sum, ring(-1))]
        return term(z + way * step) + arrived[0], term(z - way * (step - 1)) + arrived[1]

    far_sum, near_sum = step_of(term(z + way * 4), term(z - way * 3), 3)
    piece = lax.dynamic_slice(total, (core * ROWS, 0), (ROWS, 4 * ROWS))
    out = send(after(piece, [far_sum, near_sum]), to_home(0))
    far_sum, near_sum = step_of(far_sum, near_sum, 2)
    far_sum, near_sum = step_of(far_sum, near_sum, 1)
    far_sum = after(far_sum, [out])
    sums = send(far_sum, to_home(1)) + send(near_sum, to_home(0))

    offdiag = -out * mask
    labels = lax.dynamic_slice(supernode, (row * 64,), (64,))
    same = labels[:, None] == supernode[None, :]
    return offdiag, pivot_inverse + jnp.where(same, sums, 0.0)


def solution(mesh):
    in_specs = (
        P("row", "col"),
        P("row", "col"),
        P("row", "col"),
        P("col"),
        P(("col", "row"), None),
    )
    out_specs = (P("row", "col"), P(("col", "row"), None))
    return jax.shard_map(shards, mesh=mesh, in_specs=in_specs, out_specs=out_specs, check_vma=False)
```

```python
import jax
import jax.numpy as jnp
from jax import lax
from jax.experimental import pallas as pl
from jax.experimental.pallas import tpu as pltpu
from jax.sharding import PartitionSpec as P

AXES = ("col", "row")
ROWS = 256
HIGH = lax.Precision.HIGH


def place(index):
    c, r = divmod(index, 16)
    return c >> 3, (c >> 1) & 3, c & 1, r >> 1, r & 1


def index_of(xh, y, core, z, xl):
    return ((xh * 4 + y) * 2 + core) * 16 + z * 2 + xl


def pairs(move, some=lambda xh, y, core, z, xl: True):
    return [(i, index_of(*move(*place(i)))) for i in range(256) if some(*place(i))]


def ring(way):
    return pairs(
        lambda xh, y, core, z, xl: (xh, y, core, (z + (way if core == 0 else -way)) % 8, xl)
    )


def along_plane(k, axis):
    def move(xh, y, core, z, xl):
        if core == axis:
            return xh, (y + k) % 4, core, z, xl
        x = (xh * 2 + xl + k) % 4
        return x >> 1, y, core, z, x & 1

    return pairs(move)


def to_home(way):
    return pairs(
        lambda xh, y, core, z, xl: (xh, y, xl, (z + (way if core == 0 else -way)) % 8, core)
    )


def swap_cores(some=lambda xh, y, core, z, xl: True):
    return pairs(lambda xh, y, core, z, xl: (xh, y, 1 - core, z, xl), some)


def send(value, perm):
    return lax.ppermute(value, AXES, perm)


def dot(a, b):
    return jnp.dot(a, b, precision=HIGH, preferred_element_type=jnp.float32)


TILE = 256


def split(value):
    high = value.astype(jnp.bfloat16)
    return high, (value - high.astype(jnp.float32)).astype(jnp.bfloat16)


def product_kernel(count, at_ref, near_ref, *refs):
    blocks, out_ref, left_high, left_low = refs[:count], *refs[count:]

    @pl.when(pl.program_id(0) == 0)
    def _():
        for b in range(count):
            for s in range(2):
                high, low = split(near_ref[at_ref[2 * b + s]])
                left_high[pl.ds(s * ROWS, ROWS), pl.ds(b * ROWS, ROWS)] = high
                left_low[pl.ds(s * ROWS, ROWS), pl.ds(b * ROWS, ROWS)] = low

    parts = [split(block[...]) for block in blocks]
    high = jnp.concatenate([part[0] for part in parts])
    low = jnp.concatenate([part[1] for part in parts])

    def mul(a, b):
        return jnp.dot(a, b, preferred_element_type=jnp.float32)

    out_ref[...] = (
        mul(left_high[...], low) + mul(left_low[...], high) + mul(left_high[...], high)
    )


def products(at, near, blocks):
    count = len(blocks)
    columns = blocks[0].shape[1]
    return pl.pallas_call(
        lambda *refs: product_kernel(count, *refs),
        grid_spec=pltpu.PrefetchScalarGridSpec(
            num_scalar_prefetch=1,
            grid=(columns // TILE,),
            in_specs=[pl.BlockSpec(near.shape, lambda j, at: (0, 0, 0), pipeline_mode=pl.Buffered(1))]
            + [pl.BlockSpec((ROWS, TILE), lambda j, at: (0, j))] * count,
            out_specs=pl.BlockSpec((2 * ROWS, TILE), lambda j, at: (0, j)),
            scratch_shapes=[pltpu.VMEM((2 * ROWS, count * ROWS), jnp.bfloat16)] * 2,
        ),
        out_shape=jax.ShapeDtypeStruct((2 * ROWS, columns), jnp.float32),
        compiler_params=pltpu.CompilerParams(vmem_limit_bytes=24 * 2**20),
        cost_estimate=pl.CostEstimate(
            flops=6 * 2 * ROWS * count * ROWS * columns,
            bytes_accessed=4 * (near.size + count * ROWS * columns + 2 * ROWS * columns),
            transcendentals=0,
        ),
    )(at, near, *blocks)


def shards(inverse_root, factor, structure, supernode, pivot_inverse):
    col, row = lax.axis_index("col"), lax.axis_index("row")
    core, y, xh = col & 1, (col >> 1) & 3, col >> 3
    xl, z = row & 1, row >> 1
    x = xh * 2 + xl
    never = z < 0
    way = 1 - 2 * core

    def after(value, earlier):
        corner = (1,) * (value.ndim - 2) + (8, 128)
        tile = lax.slice(value, (0,) * value.ndim, corner)
        for array in earlier:
            other = lax.slice(array, (0,) * array.ndim, (1,) * (array.ndim - 2) + (8, 128))
            tile = jnp.where(never, other.reshape(corner), tile)
        return lax.dynamic_update_slice(value, tile, (0,) * value.ndim)

    spread = structure.astype(jnp.float32)[:, None, :, None]
    mask = jnp.broadcast_to(spread, (2, 128, 4, 256)).reshape(256, 1024)
    masked = factor * mask

    own = send(masked, to_home(0))
    block = after(inverse_root, [own])
    around = [send(block, along_plane(-k, 0)) for k in (1, 2, 3)]
    line = jnp.stack([block] + around)
    ahead = [own, after(send(own, ring(1)), around)]
    astern = [own, send(own, ring(-1))]
    beside = [send(line, along_plane(-1, 1)), None, send(line, along_plane(-3, 1))]
    other = send(own, swap_cores())
    ahead.append(after(send(ahead[1], ring(1)), beside[0::2] + [other]))
    astern.append(send(astern[1], ring(-1)))
    beside[1] = send(after(line, beside[0::2]), along_plane(-2, 1))
    ahead.append(after(send(ahead[2], ring(1)), beside[1:2]))
    astern.append(send(astern[2], ring(-1)))
    near = jnp.concatenate([line] + beside)

    def root_at(zk, s):
        dy = ((zk & 3) - y) & 3
        dx = (((zk & 7) >> 2) * 2 + s - x) & 3
        return jnp.where(core == 0, dx * 4 + dy, dy * 4 + dx)

    last = send(ahead[3][: ROWS // 2], ring(1))
    last_astern = send(astern[3][ROWS // 2 :], ring(-1))
    columns = jnp.where(
        core == 0, jnp.concatenate([own, other]), jnp.concatenate([other, own])
    ).T
    places = [z, z - way, z + way, z - way * 2, z + way * 2, z - way * 3, z + way * 3]
    at = jnp.stack([root_at(zk, s) for zk in places for s in range(2)])
    total = products(
        at.astype(jnp.int32),
        near,
        [own, ahead[1], astern[1], ahead[2], astern[2], ahead[3], astern[3]],
    )
    opposite = jnp.concatenate(
        [
            lax.dynamic_slice(near, (root_at(z + 4, s), 0, 0), (1, ROWS, ROWS))[0]
            for s in range(2)
        ]
    )

    total = total + dot(opposite, jnp.concatenate([last, last_astern]))
    total = total + send(total, swap_cores())

    def term(zk):
        at = (zk & 7) * 128 + core * 64
        return dot(lax.dynamic_slice(columns, (at, 0), (64, 2 * ROWS)), total)

    def step_of(far_sum, near_sum, step):
        arrived = [send(far_sum, ring(1)), send(near_sum, ring(-1))]
        return term(z + way * step) + arrived[0], term(z - way * (step - 1)) + arrived[1]

    far_sum, near_sum = step_of(term(z + way * 4), term(z - way * 3), 3)
    piece = lax.dynamic_slice(total, (core * ROWS, 0), (ROWS, 4 * ROWS))
    out = send(after(piece, [far_sum, near_sum]), to_home(0))
    far_sum, near_sum = step_of(far_sum, near_sum, 2)
    far_sum, near_sum = step_of(far_sum, near_sum, 1)
    far_sum = after(far_sum, [out])
    sums = send(far_sum, to_home(1)) + send(near_sum, to_home(0))

    offdiag = -out * mask
    labels = lax.dynamic_slice(supernode, (row * 64,), (64,))
    same = labels[:, None] == supernode[None, :]
    return offdiag, pivot_inverse + jnp.where(same, sums, 0.0)


def solution(mesh):
    in_specs = (
        P("row", "col"),
        P("row", "col"),
        P("row", "col"),
        P("col"),
        P(("col", "row"), None),
    )
    out_specs = (P("row", "col"), P(("col", "row"), None))
    return jax.shard_map(shards, mesh=mesh, in_specs=in_specs, out_specs=out_specs, check_vma=False)
```

```python
import jax
import jax.numpy as jnp
from jax import lax
from jax.experimental import pallas as pl
from jax.experimental.pallas import tpu as pltpu
from jax.sharding import PartitionSpec as P

AXES = ("col", "row")
ROWS = 256
HIGH = lax.Precision.HIGH


def place(index):
    c, r = divmod(index, 16)
    return c >> 3, (c >> 1) & 3, c & 1, r >> 1, r & 1


def index_of(xh, y, core, z, xl):
    return ((xh * 4 + y) * 2 + core) * 16 + z * 2 + xl


def pairs(move, some=lambda xh, y, core, z, xl: True):
    return [(i, index_of(*move(*place(i)))) for i in range(256) if some(*place(i))]


def ring(way):
    return pairs(
        lambda xh, y, core, z, xl: (xh, y, core, (z + (way if core == 0 else -way)) % 8, xl)
    )


def along_plane(k, axis):
    def move(xh, y, core, z, xl):
        if core == axis:
            return xh, (y + k) % 4, core, z, xl
        x = (xh * 2 + xl + k) % 4
        return x >> 1, y, core, z, x & 1

    return pairs(move)


def to_home(way):
    return pairs(
        lambda xh, y, core, z, xl: (xh, y, xl, (z + (way if core == 0 else -way)) % 8, core)
    )


def swap_cores(some=lambda xh, y, core, z, xl: True):
    return pairs(lambda xh, y, core, z, xl: (xh, y, 1 - core, z, xl), some)


def send(value, perm):
    return lax.ppermute(value, AXES, perm)


def dot(a, b):
    return jnp.dot(a, b, precision=HIGH, preferred_element_type=jnp.float32)


TILE = 256


def split(value):
    high = value.astype(jnp.bfloat16)
    return high, (value - high.astype(jnp.float32)).astype(jnp.bfloat16)


def product_kernel(count, at_ref, near_ref, *refs):
    blocks, out_ref, left_high, left_low = refs[:count], *refs[count:]

    @pl.when(pl.program_id(0) == 0)
    def _():
        for b in range(count):
            for s in range(2):
                high, low = split(near_ref[at_ref[2 * b + s]])
                left_high[pl.ds(s * ROWS, ROWS), pl.ds(b * ROWS, ROWS)] = high
                left_low[pl.ds(s * ROWS, ROWS), pl.ds(b * ROWS, ROWS)] = low

    parts = [split(block[...]) for block in blocks]
    high = jnp.concatenate([part[0] for part in parts])
    low = jnp.concatenate([part[1] for part in parts])

    def mul(a, b):
        return jnp.dot(a, b, preferred_element_type=jnp.float32)

    out_ref[...] = (
        mul(left_high[...], low) + mul(left_low[...], high) + mul(left_high[...], high)
    )


def products(at, near, blocks):
    count = len(blocks)
    columns = blocks[0].shape[1]
    return pl.pallas_call(
        lambda *refs: product_kernel(count, *refs),
        grid_spec=pltpu.PrefetchScalarGridSpec(
            num_scalar_prefetch=1,
            grid=(columns // TILE,),
            in_specs=[pl.BlockSpec(near.shape, lambda j, at: (0, 0, 0), pipeline_mode=pl.Buffered(1))]
            + [pl.BlockSpec((ROWS, TILE), lambda j, at: (0, j))] * count,
            out_specs=pl.BlockSpec((2 * ROWS, TILE), lambda j, at: (0, j)),
            scratch_shapes=[pltpu.VMEM((2 * ROWS, count * ROWS), jnp.bfloat16)] * 2,
        ),
        out_shape=jax.ShapeDtypeStruct((2 * ROWS, columns), jnp.float32),
        compiler_params=pltpu.CompilerParams(vmem_limit_bytes=24 * 2**20),
        cost_estimate=pl.CostEstimate(
            flops=6 * 2 * ROWS * count * ROWS * columns,
            bytes_accessed=4 * (near.size + count * ROWS * columns + 2 * ROWS * columns),
            transcendentals=0,
        ),
    )(at, near, *blocks)


def shards(inverse_root, factor, structure, supernode, pivot_inverse):
    col, row = lax.axis_index("col"), lax.axis_index("row")
    core, y, xh = col & 1, (col >> 1) & 3, col >> 3
    xl, z = row & 1, row >> 1
    x = xh * 2 + xl
    never = z < 0
    way = 1 - 2 * core

    def after(value, earlier):
        corner = (1,) * (value.ndim - 2) + (8, 128)
        tile = lax.slice(value, (0,) * value.ndim, corner)
        for array in earlier:
            other = lax.slice(array, (0,) * array.ndim, (1,) * (array.ndim - 2) + (8, 128))
            tile = jnp.where(never, other.reshape(corner), tile)
        return lax.dynamic_update_slice(value, tile, (0,) * value.ndim)

    spread = structure.astype(jnp.float32)[:, None, :, None]
    mask = jnp.broadcast_to(spread, (2, 128, 4, 256)).reshape(256, 1024)
    masked = factor * mask

    own = send(masked, to_home(0))
    block = after(inverse_root, [own])
    around = [send(block, along_plane(-k, 0)) for k in (1, 2, 3)]
    line = jnp.stack([block] + around)
    ahead = [own, after(send(own, ring(1)), around)]
    astern = [own, send(own, ring(-1))]
    beside = [send(line, along_plane(-1, 1)), None, send(line, along_plane(-3, 1))]
    other = send(own, swap_cores())
    ahead.append(after(send(ahead[1], ring(1)), beside[0::2] + [other]))
    astern.append(send(astern[1], ring(-1)))
    beside[1] = send(after(line, beside[0::2]), along_plane(-2, 1))
    ahead.append(after(send(ahead[2], ring(1)), beside[1:2]))
    astern.append(send(astern[2], ring(-1)))
    near = jnp.concatenate([line] + beside)

    def root_at(zk, s):
        dy = ((zk & 3) - y) & 3
        dx = (((zk & 7) >> 2) * 2 + s - x) & 3
        return jnp.where(core == 0, dx * 4 + dy, dy * 4 + dx)

    last = send(ahead[3][: ROWS // 2], ring(1))
    last_astern = send(astern[3][ROWS // 2 :], ring(-1))
    columns = jnp.where(
        core == 0, jnp.concatenate([own, other]), jnp.concatenate([other, own])
    ).T
    places = [z, z - way, z + way, z - way * 2, z + way * 2, z - way * 3, z + way * 3]
    at = jnp.stack([root_at(zk, s) for zk in places for s in range(2)])
    total = products(
        at.astype(jnp.int32),
        near,
        [own, ahead[1], astern[1], ahead[2], astern[2], ahead[3], astern[3]],
    )
    opposite = jnp.concatenate(
        [
            lax.dynamic_slice(near, (root_at(z + 4, s), 0, 0), (1, ROWS, ROWS))[0]
            for s in range(2)
        ]
    )

    total = total + dot(opposite, jnp.concatenate([last, last_astern]))
    total = total + send(total, swap_cores())

    total_high = lax.reduce_precision(total, 8, 7)
    total_low = (total - total_high).astype(jnp.bfloat16)
    total_high = total_high.astype(jnp.bfloat16)
    right = jnp.concatenate([total_high, total_low, total_high])

    def term(zk):
        at = (zk & 7) * 128 + core * 64
        left = lax.dynamic_slice(columns, (at, 0), (64, 2 * ROWS))
        high = lax.reduce_precision(left, 8, 7)
        low = (left - high).astype(jnp.bfloat16)
        high = high.astype(jnp.bfloat16)
        joined = jnp.concatenate([high, high, low], axis=1)
        return jnp.dot(joined, right, preferred_element_type=jnp.float32)

    def step_of(far_sum, near_sum, step):
        arrived = [send(far_sum, ring(1)), send(near_sum, ring(-1))]
        return term(z + way * step) + arrived[0], term(z - way * (step - 1)) + arrived[1]

    far_sum, near_sum = step_of(term(z + way * 4), term(z - way * 3), 3)
    piece = lax.dynamic_slice(total, (core * ROWS, 0), (ROWS, 4 * ROWS))
    out = send(lax.optimization_barrier((piece, far_sum, near_sum))[0], to_home(0))
    far_sum, near_sum = step_of(far_sum, near_sum, 2)
    far_sum, near_sum = step_of(far_sum, near_sum, 1)
    far_sum, out = lax.optimization_barrier((far_sum, out))
    sums = send(far_sum, to_home(1)) + send(near_sum, to_home(0))

    offdiag = -out * mask
    labels = lax.dynamic_slice(supernode, (row * 64,), (64,))
    same = labels[:, None] == supernode[None, :]
    return offdiag, pivot_inverse + jnp.where(same, sums, 0.0)


def solution(mesh):
    in_specs = (
        P("row", "col"),
        P("row", "col"),
        P("row", "col"),
        P("col"),
        P(("col", "row"), None),
    )
    out_specs = (P("row", "col"), P(("col", "row"), None))
    return jax.shard_map(shards, mesh=mesh, in_specs=in_specs, out_specs=out_specs, check_vma=False)
```

```python
import jax
import jax.numpy as jnp
from jax import lax
from jax.experimental import pallas as pl
from jax.experimental.pallas import tpu as pltpu
from jax.sharding import PartitionSpec as P

AXES = ("col", "row")
ROWS = 256
HIGH = lax.Precision.HIGH


def place(index):
    c, r = divmod(index, 16)
    return c >> 3, (c >> 1) & 3, c & 1, r >> 1, r & 1


def index_of(xh, y, core, z, xl):
    return ((xh * 4 + y) * 2 + core) * 16 + z * 2 + xl


def pairs(move, some=lambda xh, y, core, z, xl: True):
    return [(i, index_of(*move(*place(i)))) for i in range(256) if some(*place(i))]


def ring(way):
    return pairs(
        lambda xh, y, core, z, xl: (xh, y, core, (z + (way if core == 0 else -way)) % 8, xl)
    )


def along_plane(k, axis):
    def move(xh, y, core, z, xl):
        if core == axis:
            return xh, (y + k) % 4, core, z, xl
        x = (xh * 2 + xl + k) % 4
        return x >> 1, y, core, z, x & 1

    return pairs(move)


def to_home(way):
    return pairs(
        lambda xh, y, core, z, xl: (xh, y, xl, (z + (way if core == 0 else -way)) % 8, core)
    )


def swap_cores(some=lambda xh, y, core, z, xl: True):
    return pairs(lambda xh, y, core, z, xl: (xh, y, 1 - core, z, xl), some)


def send(value, perm):
    return lax.ppermute(value, AXES, perm)


def dot(a, b):
    return jnp.dot(a, b, precision=HIGH, preferred_element_type=jnp.float32)


TILE = 256


def split(value):
    high = value.astype(jnp.bfloat16)
    return high, (value - high.astype(jnp.float32)).astype(jnp.bfloat16)


def product_kernel(count, at_ref, near_ref, *refs):
    blocks, out_ref, left_high, left_low = refs[:count], *refs[count:]

    @pl.when(pl.program_id(0) == 0)
    def _():
        for b in range(count):
            for s in range(2):
                high, low = split(near_ref[at_ref[2 * b + s]])
                left_high[pl.ds(s * ROWS, ROWS), pl.ds(b * ROWS, ROWS)] = high
                left_low[pl.ds(s * ROWS, ROWS), pl.ds(b * ROWS, ROWS)] = low

    parts = [split(block[...]) for block in blocks]
    high = jnp.concatenate([part[0] for part in parts])
    low = jnp.concatenate([part[1] for part in parts])

    def mul(a, b):
        return jnp.dot(a, b, preferred_element_type=jnp.float32)

    out_ref[...] = (
        mul(left_high[...], low) + mul(left_low[...], high) + mul(left_high[...], high)
    )


def products(at, near, blocks):
    count = len(blocks)
    columns = blocks[0].shape[1]
    return pl.pallas_call(
        lambda *refs: product_kernel(count, *refs),
        grid_spec=pltpu.PrefetchScalarGridSpec(
            num_scalar_prefetch=1,
            grid=(columns // TILE,),
            in_specs=[pl.BlockSpec(near.shape, lambda j, at: (0, 0, 0), pipeline_mode=pl.Buffered(1))]
            + [pl.BlockSpec((ROWS, TILE), lambda j, at: (0, j))] * count,
            out_specs=pl.BlockSpec((2 * ROWS, TILE), lambda j, at: (0, j)),
            scratch_shapes=[pltpu.VMEM((2 * ROWS, count * ROWS), jnp.bfloat16)] * 2,
        ),
        out_shape=jax.ShapeDtypeStruct((2 * ROWS, columns), jnp.float32),
        compiler_params=pltpu.CompilerParams(vmem_limit_bytes=24 * 2**20),
        cost_estimate=pl.CostEstimate(
            flops=6 * 2 * ROWS * count * ROWS * columns,
            bytes_accessed=4 * (near.size + count * ROWS * columns + 2 * ROWS * columns),
            transcendentals=0,
        ),
    )(at, near, *blocks)


def shards(inverse_root, factor, structure, supernode, pivot_inverse):
    col, row = lax.axis_index("col"), lax.axis_index("row")
    core, y, xh = col & 1, (col >> 1) & 3, col >> 3
    xl, z = row & 1, row >> 1
    x = xh * 2 + xl
    never = z < 0
    way = 1 - 2 * core

    def after(value, earlier):
        corner = (1,) * (value.ndim - 2) + (8, 128)
        tile = lax.slice(value, (0,) * value.ndim, corner)
        for array in earlier:
            other = lax.slice(array, (0,) * array.ndim, (1,) * (array.ndim - 2) + (8, 128))
            tile = jnp.where(never, other.reshape(corner), tile)
        return lax.dynamic_update_slice(value, tile, (0,) * value.ndim)

    spread = structure.astype(jnp.float32)[:, None, :, None]
    mask = jnp.broadcast_to(spread, (2, 128, 4, 256)).reshape(256, 1024)
    masked = factor * mask

    own = send(masked, to_home(0))
    block = after(inverse_root, [own])
    around = [send(block, along_plane(-k, 0)) for k in (1, 2, 3)]
    line = jnp.stack([block] + around)
    ahead = [own, after(send(own, ring(1)), around)]
    astern = [own, send(own, ring(-1))]
    beside = [send(line, along_plane(-1, 1)), None, send(line, along_plane(-3, 1))]
    other = send(own, swap_cores())
    ahead.append(after(send(ahead[1], ring(1)), beside[0::2]))
    astern.append(send(astern[1], ring(-1)))
    beside[1] = send(after(line, beside[0::2]), along_plane(-2, 1))
    ahead.append(after(send(ahead[2], ring(1)), beside[1:2] + [other]))
    astern.append(send(astern[2], ring(-1)))
    near = jnp.concatenate([line] + beside)

    def root_at(zk, s):
        dy = ((zk & 3) - y) & 3
        dx = (((zk & 7) >> 2) * 2 + s - x) & 3
        return jnp.where(core == 0, dx * 4 + dy, dy * 4 + dx)

    last = send(ahead[3][: ROWS // 2], ring(1))
    last_astern = send(astern[3][ROWS // 2 :], ring(-1))
    columns = jnp.where(
        core == 0, jnp.concatenate([own, other]), jnp.concatenate([other, own])
    ).T
    places = [z, z - way, z + way, z - way * 2, z + way * 2, z - way * 3, z + way * 3]
    at = jnp.stack([root_at(zk, s) for zk in places for s in range(2)])
    total = products(
        at.astype(jnp.int32),
        near,
        [own, ahead[1], astern[1], ahead[2], astern[2], ahead[3], astern[3]],
    )
    opposite = jnp.concatenate(
        [
            lax.dynamic_slice(near, (root_at(z + 4, s), 0, 0), (1, ROWS, ROWS))[0]
            for s in range(2)
        ]
    )

    total = total + dot(opposite, jnp.concatenate([last, last_astern]))
    total = total + send(total, swap_cores())

    total_high = lax.reduce_precision(total, 8, 7)
    total_low = (total - total_high).astype(jnp.bfloat16)
    total_high = total_high.astype(jnp.bfloat16)
    right = jnp.concatenate([total_high, total_low, total_high])

    def term(zk):
        at = (zk & 7) * 128 + core * 64
        left = lax.dynamic_slice(columns, (at, 0), (64, 2 * ROWS))
        high = lax.reduce_precision(left, 8, 7)
        low = (left - high).astype(jnp.bfloat16)
        high = high.astype(jnp.bfloat16)
        joined = jnp.concatenate([high, high, low], axis=1)
        return jnp.dot(joined, right, preferred_element_type=jnp.float32)

    def step_of(far_sum, near_sum, step):
        arrived = [send(far_sum, ring(1)), send(near_sum, ring(-1))]
        return term(z + way * step) + arrived[0], term(z - way * (step - 1)) + arrived[1]

    far_sum, near_sum = step_of(term(z + way * 4), term(z - way * 3), 3)
    piece = lax.dynamic_slice(total, (core * ROWS, 0), (ROWS, 4 * ROWS))
    out = send(lax.optimization_barrier((piece, far_sum, near_sum))[0], to_home(0))
    far_sum, near_sum = step_of(far_sum, near_sum, 2)
    far_sum, near_sum = step_of(far_sum, near_sum, 1)
    far_sum, out = lax.optimization_barrier((far_sum, out))
    sums = send(far_sum, to_home(1)) + send(near_sum, to_home(0))

    offdiag = -out * mask
    labels = lax.dynamic_slice(supernode, (row * 64,), (64,))
    same = labels[:, None] == supernode[None, :]
    return offdiag, pivot_inverse + jnp.where(same, sums, 0.0)


def solution(mesh):
    in_specs = (
        P("row", "col"),
        P("row", "col"),
        P("row", "col"),
        P("col"),
        P(("col", "row"), None),
    )
    out_specs = (P("row", "col"), P(("col", "row"), None))
    return jax.shard_map(shards, mesh=mesh, in_specs=in_specs, out_specs=out_specs, check_vma=False)
```
